512 devices in a mesh: patch: 32 (over z_hi, x, core), uly: 16 (over z_lo, y).
Axes of the slice: x: 4, y: 8, z: 8 (z_hi: 4, z_lo: 2; z = z_hi * 2 + z_lo), core: 2. Of those that a mesh axis runs over, the one named last changes fastest.
Arguments:
- queries: bfloat16 [8192, 6144], P(('patch', 'uly')), may hold values from -18 to 18
- keys: bfloat16 [8192, 6144], P(('patch', 'uly')), may hold values from -18 to 18
- values: bfloat16 [8192, 6144], P(('patch', 'uly')), may hold values from -12 to 12
- stale_cache: bfloat16 [2, 8192, 6144], P(None, 'patch', 'uly'), may hold values from -14 to 14
Outputs:
- attended: bfloat16 [8192, 6144], P(('patch', 'uly'))
- fresh_cache: bfloat16 [2, 8192, 6144], P(None, 'patch', 'uly')
The draws below stay inside these ranges and needn't reach their ends.
All inputs are finite; a program needn't handle non-finite values.
Results may differ from the reference program's by a relative error of at most 0.0055.
Values may be sent and summed in bfloat16 or wider, within the bound.
A program may use at most 128 MiB of HBM per device.

```python
import jax
import jax.numpy as jnp
from jax import lax

HEADS = 48
HEAD_DIM = 128
PATCH_TOK = 256
D = 6144
TOKENS = 8192


def row_scales(key, lower, upper):
    return jnp.exp(jax.random.uniform(key, (TOKENS, 1), jnp.float32, jnp.log(lower), jnp.log(upper)))


def draw_queries(key, part):
    key = jax.random.fold_in(key, 1)
    base_key, scale_key = jax.random.split(key)
    base = jnp.clip(jax.random.normal(base_key, (TOKENS, HEADS * HEAD_DIM), jnp.float32), -4.5, 4.5)
    result = base * row_scales(scale_key, 2.5, 4.0)
    return result.astype(jnp.bfloat16)


def draw_keys(key, part):
    key = jax.random.fold_in(key, 2)
    base_key, scale_key = jax.random.split(key)
    base = jnp.clip(jax.random.normal(base_key, (TOKENS, HEADS * HEAD_DIM), jnp.float32), -4.5, 4.5)
    result = base * row_scales(scale_key, 0.4, 0.7)
    return result.astype(jnp.bfloat16)


def draw_stale_cache(key, part):
    key = jax.random.fold_in(key, 3)
    key_part, value_part, scale_key = jax.random.split(key, 3)
    cached_keys = jnp.clip(jax.random.normal(key_part, (TOKENS, HEADS * HEAD_DIM), jnp.float32), -4.5, 4.5)
    cached_keys = cached_keys * row_scales(scale_key, 0.4, 0.7)
    cached_values = 2.0 * jnp.clip(jax.random.normal(value_part, (TOKENS, HEADS * HEAD_DIM), jnp.float32), -6.0, 6.0)
    return jnp.stack([cached_keys, cached_values]).astype(jnp.bfloat16)


def shard_levels(rng, extent, pieces, least, high):
    factor_of = 1.0
    for position, shards_of in pieces:
        steps = jax.random.uniform(jax.random.fold_in(jax.random.fold_in(rng, 6), position), (shards_of,), jnp.float32, least / len(pieces), high / len(pieces))
        factor_of = factor_of * jnp.repeat(jnp.exp(steps), extent[position] // shards_of).reshape((-1,) + (1,) * (len(extent) - 1 - position))
    return factor_of


def centred(stream_key, dims, deviation, reach, cuts=(), kind=jnp.bfloat16):
    drawn = jax.random.normal(stream_key, dims, jnp.float32) * deviation
    if len(cuts) > 0:
        drawn = shard_levels(stream_key, dims, cuts, -0.22, 0.18) * drawn
    return jnp.clip(drawn, min=-reach, max=reach).astype(kind)


def setup_inputs(seed: int = 0) -> dict:
    key_list = jax.random.split(jax.random.key(seed), 5)
    return {
        "queries": draw_queries(jax.random.fold_in(key_list[4], 71), 0),
        "keys": draw_keys(jax.random.fold_in(key_list[4], 71), 0),
        "values": centred(key_list[2], (TOKENS, D), 2.0, 12.0, ((0, 512),)),
        "stale_cache": draw_stale_cache(jax.random.fold_in(key_list[4], 71), 0),
    }


def reference(queries, keys, values, stale_cache):
    score_scale = HEAD_DIM ** -0.5
    patch_count = TOKENS // PATCH_TOK
    zero_index = jnp.zeros((), jnp.int32)

    def patch_output(patch_index):
        first_row = (patch_index * PATCH_TOK).astype(jnp.int32)

        def head_output(head_index):
            column = (head_index * HEAD_DIM).astype(jnp.int32)
            query_rows = lax.dynamic_slice(queries, (first_row, column), (PATCH_TOK, HEAD_DIM))
            fresh_keys = lax.dynamic_slice(keys, (first_row, column), (PATCH_TOK, HEAD_DIM))
            fresh_values = lax.dynamic_slice(values, (first_row, column), (PATCH_TOK, HEAD_DIM))
            key_rows = lax.dynamic_slice(stale_cache[0], (zero_index, column), (TOKENS, HEAD_DIM))
            value_rows = lax.dynamic_slice(stale_cache[1], (zero_index, column), (TOKENS, HEAD_DIM))
            key_rows = lax.dynamic_update_slice(key_rows, fresh_keys, (first_row, zero_index))
            value_rows = lax.dynamic_update_slice(value_rows, fresh_values, (first_row, zero_index))
            scores = jnp.dot(query_rows, key_rows.T, preferred_element_type=jnp.float32) * score_scale
            weights = jnp.exp(scores - jnp.max(scores, axis=1, keepdims=True))
            totals = jnp.sum(weights, axis=1, keepdims=True)
            numerators = jnp.dot(weights.astype(jnp.bfloat16), value_rows, preferred_element_type=jnp.float32)
            return (numerators / totals).astype(jnp.bfloat16)

        return lax.map(head_output, jnp.arange(HEADS, dtype=jnp.int32))

    outputs = lax.map(patch_output, jnp.arange(patch_count, dtype=jnp.int32))
    attended = jnp.transpose(outputs, (0, 2, 1, 3)).reshape(TOKENS, HEADS * HEAD_DIM)
    fresh_cache = jnp.stack([keys, values])
    return attended, fresh_cache
```

```python
import jax
import jax.numpy as jnp
from jax import lax
from jax.experimental import pallas as pl
from jax.experimental.pallas import tpu as pltpu
from jax.sharding import PartitionSpec as P

MESH = pl.DeviceIdType.MESH
HEADS = 48
HD = 128
SCALE = 1.4426950408889634 * HD**-0.5

KINDS = (
    [(t, r) for t in "KV" for r in ("z", "x", "s0", "xz", "s1", "s2", "s3")]
    + [("Q", r) for r in ("z", "x", "xz")]
    + [(t, r) for t in "OT" for r in (0, 1, 2)]
)
KIND_INDEX = {kind: i for i, kind in enumerate(KINDS)}


def kernel(
    q_hbm, k_hbm, v_hbm, stale, out, fresh,
    ka, va, qa, qland, kland, vland, stale_v,
    scores, part_o, part_t, send_o, send_t, got_o, got_t, final,
    ssem, rsem, a2a_s, a2a_r, ao_s, ao_r, lsem,
):
    rows, width = q_hbm.shape
    uly = width // qland.shape[1]
    nh = qland.shape[1] // HD
    patch = lax.axis_index("patch")
    me = lax.axis_index("uly")
    core = patch % 2
    x = (patch // 2) % 4
    zh = patch // 8

    def at_patch(zh_, x_, core_):
        return ((zh_ * 4 + x_) * 2 + core_, me)

    sib = at_patch(zh, x, 1 - core)
    zk = at_patch(zh + 1 - 2 * (zh % 2), x, core)
    xk = at_patch(zh, x + 1 - 2 * (x % 2), core)
    zq = at_patch(3 - zh, x, core)
    xq = at_patch(zh, 3 - x, core)

    def copy(kind, h):
        t, r = kind
        if t in "KV":
            slots = ka if t == "K" else va
            own = slots.at[0, h]
            src, dst, to = {
                "z": (own, 1, zk),
                "x": (own, 2, xk),
                "s0": (own, 4, sib),
                "xz": (slots.at[1, h], 3, xk),
                "s1": (slots.at[1, h], 5, sib),
                "s2": (slots.at[2, h], 6, sib),
                "s3": (slots.at[3, h], 7, sib),
            }[r]
            dst = slots.at[dst, h]
        elif t == "Q":
            src, dst, to = {"z": (3, 2, zq), "x": (3, 1, xq), "xz": (2, 0, xq)}[r]
            src, dst = qa.at[src, h], qa.at[dst, h]
        else:
            src = (send_o if t == "O" else send_t).at[h, r]
            dst = (got_o if t == "O" else got_t).at[h, r]
            to = zq if r == 2 else xq
        i = KIND_INDEX[kind] * nh + h
        return pltpu.make_async_remote_copy(
            src_ref=src, dst_ref=dst, send_sem=ssem.at[i], recv_sem=rsem.at[i],
            device_id=to, device_id_type=MESH,
        )

    def start(t, r, h):
        copy((t, r), h).start()

    def arrived(t, r, h):
        copy((t, r), h).wait_recv()

    cut = pl.ds(pl.multiple_of(me * nh * HD, HD), nh * HD)
    mine = pl.ds(pl.multiple_of(me * rows, rows), rows)
    local = [pltpu.make_async_copy(stale.at[1], stale_v, lsem.at[0])]
    for i, (src, dst) in enumerate(((q_hbm, qland), (k_hbm, kland), (v_hbm, vland))):
        local.append(pltpu.make_async_copy(src.at[:, cut], dst.at[mine], lsem.at[1 + i]))
    for h in range(nh):
        local.append(
            pltpu.make_async_copy(stale.at[0, :, pl.ds(h * HD, HD)], ka.at[0, h], lsem.at[4 + h])
        )
    for c in local:
        c.start()

    barrier = pltpu.get_barrier_semaphore()
    for i in range(1, uly):
        pl.semaphore_signal(
            barrier, inc=1, device_id=(patch, (me + i) % uly), device_id_type=MESH
        )
    for to in (sib, zk, xk, zq, xq):
        pl.semaphore_signal(barrier, inc=1, device_id=to, device_id_type=MESH)

    local[0].wait()
    for h in range(nh):
        va[0, h] = stale_v[:, h * HD : (h + 1) * HD].T
    for h in range(nh):
        local[4 + h].wait()
    pl.semaphore_wait(barrier, uly - 1 + 5)

    def exchange(n, src, dst):
        for i in range(1, uly):
            peer = (me + i) % uly
            pltpu.make_async_remote_copy(
                src_ref=src.at[:, pl.ds(pl.multiple_of(peer * nh * HD, HD), nh * HD)],
                dst_ref=dst.at[mine],
                send_sem=a2a_s.at[n], recv_sem=a2a_r.at[n],
                device_id=(patch, peer), device_id_type=MESH,
            ).start()

    def exchanged(n, dst):
        whole = dst.at[pl.ds(0, (uly - 1) * rows)]
        pltpu.make_async_copy(whole, whole, a2a_r.at[n]).wait()
        local[1 + n].wait()

    exchange(0, q_hbm, qland)
    for h in range(nh):
        for t in "KV":
            start(t, "z", h)
            start(t, "x", h)
            start(t, "s0", h)
    exchange(1, k_hbm, kland)
    exchange(2, v_hbm, vland)
    exchanged(0, qland)
    for h in range(nh):
        qa[3, h] = qland[:, h * HD : (h + 1) * HD]
        start("Q", "z", h)
        start("Q", "x", h)

    def forward_z(t, h):
        arrived(t, "z", h)
        start(t, "xz", h)
        start(t, "s1", h)

    def forward_x(h):
        arrived("Q", "z", h)
        start("Q", "xz", h)
        for t in "KV":
            arrived(t, "x", h)
            start(t, "s2", h)

    def forward_xz(h):
        for t in "KV":
            arrived(t, "xz", h)
            start(t, "s3", h)

    def ready(h):
        for t in "KV":
            for r in ("s0", "s1", "s2", "s3"):
                arrived(t, r, h)
        arrived("Q", "x", h)
        arrived("Q", "xz", h)

    def take_fresh():
        exchanged(1, kland)
        exchanged(2, vland)
        pltpu.make_async_copy(kland, fresh.at[0], lsem.at[7]).start()
        pltpu.make_async_copy(vland, fresh.at[1], lsem.at[8]).start()
        for h in range(nh):
            ka[8, h] = kland[:, h * HD : (h + 1) * HD]
            va[8, h] = vland[:, h * HD : (h + 1) * HD].T

    def stats(m, l):
        row = lax.broadcasted_iota(jnp.int32, (8, m.shape[1]), 0)
        return jnp.where(row < 4, jnp.broadcast_to(m, row.shape), jnp.broadcast_to(l, row.shape))

    def combine(o1, t1, o2, t2):
        m1, l1, m2, l2 = t1[0:1], t1[4:5], t2[0:1], t2[4:5]
        m = jnp.maximum(m1, m2)
        a1 = l1 * jnp.exp2((m1 - m) * SCALE)
        a2 = l2 * jnp.exp2((m2 - m) * SCALE)
        l = a1 + a2
        return o1 * (a1 / l) + o2.astype(jnp.float32) * (a2 / l), stats(m, l)

    def combine_x(h):
        arrived("O", 0, h)
        arrived("T", 0, h)
        o, t = combine(part_o[h, 0], part_t[h, 0], got_o[h, 0], got_t[h, 0])
        send_o[h, 2] = o.astype(jnp.bfloat16)
        send_t[h, 2] = t
        start("O", 2, h)
        start("T", 2, h)
        arrived("O", 1, h)
        arrived("T", 1, h)
        o, t = combine(part_o[h, 1], part_t[h, 1], got_o[h, 1], got_t[h, 1])
        part_o[h, 1] = o
        part_t[h, 1] = t

    def out_columns(h):
        return pl.ds(pl.multiple_of((me * nh + h) * HD, HD), HD)

    def combine_z(h):
        arrived("O", 2, h)
        arrived("T", 2, h)
        o, _ = combine(part_o[h, 1], part_t[h, 1], got_o[h, 2], got_t[h, 2])
        final[h] = o.T.astype(jnp.bfloat16)
        pltpu.make_async_copy(final.at[h, mine], out.at[:, out_columns(h)], lsem.at[9 + h]).start()
        for i in range(1, uly):
            peer = (me + i) % uly
            pltpu.make_async_remote_copy(
                src_ref=final.at[h, pl.ds(pl.multiple_of(peer * rows, rows), rows)],
                dst_ref=out.at[:, out_columns(h)],
                send_sem=ao_s.at[h], recv_sem=ao_r.at[h],
                device_id=(patch, peer), device_id_type=MESH,
            ).start()

    def prepare(h):
        forward_z("K", h)
        forward_z("V", h)
        forward_x(h)
        forward_xz(h)
        ready(h)

    plan = {
        0: lambda: prepare(0),
        1: lambda: forward_z("K", 1),
        2: lambda: (forward_z("V", 1), forward_x(1)),
        3: take_fresh,
        4: lambda: (forward_xz(1), ready(1)),
        5: lambda: (forward_z("K", 2), combine_x(0)),
        6: lambda: (forward_z("V", 2), forward_x(2)),
        7: lambda: combine_z(0),
        8: lambda: (forward_xz(2), ready(2)),
        9: lambda: combine_x(1),
        11: lambda: combine_z(1),
    }
    blk = ka.shape[2]

    def attend(h, j):
        q = qa[j, h]
        first = (j // 3) * 8
        m8 = None
        for b in range(8):
            k = ka[first if b == 0 else b, h]
            s = lax.dot_general(k, q, (((1,), (1,)), ((), ())), preferred_element_type=jnp.float32)
            scores[b * blk : (b + 1) * blk] = s
            top = jnp.max(s.reshape(blk // 8, 8, s.shape[1]), axis=0)
            m8 = top if m8 is None else jnp.maximum(m8, top)
        m = jnp.max(m8, axis=0, keepdims=True)
        l8 = jnp.zeros_like(m8)
        acc = jnp.zeros((HD, q.shape[0]), jnp.float32)
        for b in range(8):
            w = jnp.exp2((scores[b * blk : (b + 1) * blk] - m) * SCALE)
            l8 = l8 + jnp.sum(w.reshape(blk // 8, 8, w.shape[1]), axis=0)
            acc = acc + jnp.dot(
                va[first if b == 0 else b, h], w.astype(jnp.bfloat16),
                preferred_element_type=jnp.float32,
            )
        l = jnp.sum(l8, axis=0, keepdims=True)
        return acc * (1.0 / l), stats(m, l)

    def step(s, _):
        for at, action in plan.items():
            pl.when(s == at)(lambda action=action: (action(), None)[1])
        h, j = s // 4, s % 4
        o, t = attend(h, j)

        @pl.when(j < 2)
        def _():
            send_o[h, j] = o.astype(jnp.bfloat16)
            send_t[h, j] = t

        for r in (0, 1):

            @pl.when(j == r)
            def _(r=r):
                start("O", r, h)
                start("T", r, h)

        @pl.when(j >= 2)
        def _():
            part_o[h, j - 2] = o
            part_t[h, j - 2] = t

        return 0

    lax.fori_loop(0, 4 * nh, step, 0)
    combine_x(nh - 1)
    combine_z(nh - 1)

    for h in range(nh):
        some = out.at[:, pl.ds(0, (uly - 1) * HD)]
        pltpu.make_async_copy(some, some, ao_r.at[h]).wait()
        pltpu.make_async_copy(some, some, ao_s.at[h]).wait()
        pltpu.make_async_copy(final.at[h, mine], out.at[:, out_columns(h)], lsem.at[9 + h]).wait()
    for n, dst in enumerate((qland, kland, vland)):
        whole = dst.at[pl.ds(0, (uly - 1) * rows)]
        pltpu.make_async_copy(whole, whole, a2a_s.at[n]).wait()
    pltpu.make_async_copy(kland, fresh.at[0], lsem.at[7]).wait()
    pltpu.make_async_copy(vland, fresh.at[1], lsem.at[8]).wait()
    for kind in KINDS:
        for h in range(nh):
            copy(kind, h).wait_send()


def local(queries, keys, values, stale_cache):
    rows, width = queries.shape
    _, patch_rows, cols = stale_cache.shape
    nh = cols // HD
    bf, f32 = jnp.bfloat16, jnp.float32
    n_copies = len(KINDS) * nh
    vm = pltpu.VMEM
    dma = pltpu.SemaphoreType.DMA
    return pl.pallas_call(
        kernel,
        out_shape=(
            jax.ShapeDtypeStruct((rows, width), bf),
            jax.ShapeDtypeStruct(stale_cache.shape, bf),
        ),
        in_specs=[pl.BlockSpec(memory_space=pl.ANY)] * 4,
        out_specs=(pl.BlockSpec(memory_space=pl.ANY),) * 2,
        scratch_shapes=[
            vm((9, nh, patch_rows, HD), bf),
            vm((9, nh, HD, patch_rows), bf),
            vm((4, nh, patch_rows, HD), bf),
            vm((patch_rows, cols), bf),
            vm((patch_rows, cols), bf),
            vm((patch_rows, cols), bf),
            vm((patch_rows, cols), bf),
            vm((8 * patch_rows, patch_rows), f32),
            vm((nh, 2, HD, patch_rows), f32),
            vm((nh, 2, 8, patch_rows), f32),
            vm((nh, 3, HD, patch_rows), bf),
            vm((nh, 3, 8, patch_rows), f32),
            vm((nh, 3, HD, patch_rows), bf),
            vm((nh, 3, 8, patch_rows), f32),
            vm((nh, patch_rows, HD), bf),
            dma((n_copies,)),
            dma((n_copies,)),
            dma((3,)),
            dma((3,)),
            dma((nh,)),
            dma((nh,)),
            dma((9 + nh,)),
        ],
        compiler_params=pltpu.CompilerParams(
            collective_id=0, has_side_effects=True, vmem_limit_bytes=40 * 2**20
        ),
        cost_estimate=pl.CostEstimate(
            flops=4 * 8 * 4 * patch_rows**2 * cols,
            bytes_accessed=8 * patch_rows * cols,
            transcendentals=32 * patch_rows**2 * nh,
        ),
    )(queries, keys, values, stale_cache)


def solution(mesh):
    in_specs = (
        P(("patch", "uly"), None),
        P(("patch", "uly"), None),
        P(("patch", "uly"), None),
        P(None, "patch", "uly"),
    )
    out_specs = (P(("patch", "uly"), None), P(None, "patch", "uly"))
    return jax.shard_map(local, mesh=mesh, in_specs=in_specs, out_specs=out_specs, check_vma=False)
```

```python
import jax
import jax.numpy as jnp
from jax import lax
from jax.experimental import pallas as pl
from jax.experimental.pallas import tpu as pltpu
from jax.sharding import PartitionSpec as P

MESH = pl.DeviceIdType.MESH
HEADS = 48
HD = 128
SCALE = 1.4426950408889634 * HD**-0.5

KINDS = (
    [(t, r) for t in "KV" for r in ("z", "x", "s0", "xz", "s1", "s2", "s3")]
    + [("Q", r) for r in ("z", "x", "xz")]
    + [(t, r) for t in "OT" for r in (0, 1, 2)]
)
KIND_INDEX = {kind: i for i, kind in enumerate(KINDS)}


def kernel(
    q_hbm, k_hbm, v_hbm, stale, out, fresh,
    ka, va, qa, qland, kland, vland, stale_v,
    scores, part_o, part_t, send_o, send_t, got_o, got_t, final,
    ssem, rsem, a2a_s, a2a_r, ao_s, ao_r, lsem,
):
    rows, width = q_hbm.shape
    uly = width // qland.shape[1]
    nh = qland.shape[1] // HD
    patch = lax.axis_index("patch")
    me = lax.axis_index("uly")
    core = patch % 2
    x = (patch // 2) % 4
    zh = patch // 8

    def at_patch(zh_, x_, core_):
        return ((zh_ * 4 + x_) * 2 + core_, me)

    sib = at_patch(zh, x, 1 - core)

    def flip(i, crossed):
        return (i + 1 - 2 * (i % 2)) * (1 - crossed) + (3 - i) * crossed

    def partner(r, crossed):
        return at_patch(
            flip(zh, crossed) if "z" in r else zh, flip(x, crossed) if "x" in r else x, core
        )

    def copy(kind, h):
        t, r = kind
        if t in "KV":
            slots = ka if t == "K" else va
            src, dst, to = {
                "z": (0, 1, "z"),
                "x": (0, 2, "x"),
                "s0": (0, 4, ""),
                "xz": (1, 3, "x"),
                "s1": (1, 5, ""),
                "s2": (2, 6, ""),
                "s3": (3, 7, ""),
            }[r]
            if t == "K" and src == 0:
                src = stale.at[0, :, pl.ds(h * HD, HD)]
            else:
                src = slots.at[src, h]
            dst = slots.at[dst, h]
            to = partner(to, h % 2) if to else sib
        elif t == "Q":
            src, dst = qa.at[3, h], qa.at[("xz", "x", "z").index(r), h]
            to = partner(r, 1 - h % 2)
        else:
            src = (send_o if t == "O" else send_t).at[h, r]
            dst = (got_o if t == "O" else got_t).at[h, r]
            to = partner(("xz", "x", "z")[r], 1 - h % 2)
        i = KIND_INDEX[kind] * nh + h
        return pltpu.make_async_remote_copy(
            src_ref=src, dst_ref=dst, send_sem=ssem.at[i], recv_sem=rsem.at[i],
            device_id=to, device_id_type=MESH,
        )

    def start(t, r, h):
        copy((t, r), h).start()

    def arrived(t, r, h):
        copy((t, r), h).wait_recv()

    barrier = pltpu.get_barrier_semaphore()
    ring = uly // 2
    steps = [(dz, dy) for dz in range(2) for dy in range(ring) if dz + dy]
    steps.sort(key=lambda d: -d[0] - min(d[1], ring - d[1]))
    peers = [((me // ring + dz) % 2) * ring + (me + dy) % ring for dz, dy in steps]
    for peer in peers:
        pl.semaphore_signal(barrier, inc=1, device_id=(patch, peer), device_id_type=MESH)
    near = [sib] + [partner(r, crossed) for r in ("z", "x", "xz") for crossed in (0, 1)]
    for to in near:
        pl.semaphore_signal(barrier, inc=1, device_id=to, device_id_type=MESH)

    cut = pl.ds(pl.multiple_of(me * nh * HD, HD), nh * HD)
    mine = pl.ds(pl.multiple_of(me * rows, rows), rows)
    local = [pltpu.make_async_copy(stale.at[1], stale_v, lsem.at[0])]
    for i, (src, dst) in enumerate(((q_hbm, qland), (k_hbm, kland), (v_hbm, vland))):
        local.append(pltpu.make_async_copy(src.at[:, cut], dst.at[mine], lsem.at[1 + i]))
    for h in range(nh):
        local.append(
            pltpu.make_async_copy(stale.at[0, :, pl.ds(h * HD, HD)], ka.at[0, h], lsem.at[4 + h])
        )
    for c in local:
        c.start()

    pl.semaphore_wait(barrier, uly - 1 + len(near))

    def exchange(n, src, dst):
        for peer in peers:
            pltpu.make_async_remote_copy(
                src_ref=src.at[:, pl.ds(pl.multiple_of(peer * nh * HD, HD), nh * HD)],
                dst_ref=dst.at[mine],
                send_sem=a2a_s.at[n], recv_sem=a2a_r.at[n],
                device_id=(patch, peer), device_id_type=MESH,
            ).start()

    def exchanged(n, dst):
        whole = dst.at[pl.ds(0, (uly - 1) * rows)]
        pltpu.make_async_copy(whole, whole, a2a_r.at[n]).wait()
        local[1 + n].wait()

    def forward_z(t, h):
        arrived(t, "z", h)
        start(t, "xz", h)
        start(t, "s1", h)

    def forward_x(t, h):
        arrived(t, "x", h)
        start(t, "s2", h)

    def forward_xz(t, h):
        arrived(t, "xz", h)
        start(t, "s3", h)

    def ready(t, h):
        for r in ("s0", "s1", "s2", "s3"):
            arrived(t, r, h)

    def start_both(r, h):
        for t in "KV":
            start(t, r, h)

    def start_query(h):
        qa[3, h] = qland[:, h * HD : (h + 1) * HD]
        for r in ("xz", "z", "x"):
            start("Q", r, h)

    exchange(0, q_hbm, qland)
    for h in (0, 1):
        for r in ("z", "x", "s0"):
            start("K", r, h)
    local[0].wait()
    for h in range(nh):
        va[0, h] = stale_v[:, h * HD : (h + 1) * HD].T
        if h < 2:
            for r in ("z", "x", "s0"):
                start("V", r, h)
    for h in range(nh):
        local[4 + h].wait()
    for t in "KV":
        forward_z(t, 0)
    start_both("z", 2)
    for t in "KV":
        forward_z(t, 1)
    for h in (0, 1):
        for t in "KV":
            forward_x(t, h)
    exchanged(0, qland)
    start_query(0)
    start_query(1)
    start_query(2)
    exchange(1, k_hbm, kland)
    exchange(2, v_hbm, vland)
    for t in "KV":
        forward_xz(t, 0)
    start_both("x", 2)
    start_both("s0", 2)
    for t in "KV":
        forward_xz(t, 1)
    ready("K", 0)
    arrived("Q", "x", 0)

    def take_fresh():
        exchanged(1, kland)
        exchanged(2, vland)
        pltpu.make_async_copy(kland, fresh.at[0], lsem.at[7]).start()
        pltpu.make_async_copy(vland, fresh.at[1], lsem.at[8]).start()
        for h in range(nh):
            ka[8, h] = kland[:, h * HD : (h + 1) * HD]
            va[8, h] = vland[:, h * HD : (h + 1) * HD].T

    def stats(m, l):
        row = lax.broadcasted_iota(jnp.int32, (8, m.shape[1]), 0)
        return jnp.where(row < 4, jnp.broadcast_to(m, row.shape), jnp.broadcast_to(l, row.shape))

    def out_columns(h):
        return pl.ds(pl.multiple_of((me * nh + h) * HD, HD), HD)

    def finish(h):
        for r in range(3):
            arrived("O", r, h)
            arrived("T", r, h)
        ts = [part_t[h]] + [got_t[h, r] for r in range(3)]
        m = jnp.maximum(
            jnp.maximum(ts[0][0:1], ts[1][0:1]), jnp.maximum(ts[2][0:1], ts[3][0:1])
        )
        shares = [t[4:5] * jnp.exp2((t[0:1] - m) * SCALE) for t in ts]
        inverse = 1.0 / (shares[0] + shares[1] + shares[2] + shares[3])
        o = part_o[h] * (shares[0] * inverse)
        for r in range(3):
            o = o + got_o[h, r].astype(jnp.float32) * (shares[1 + r] * inverse)
        final[h] = o.T.astype(jnp.bfloat16)
        pltpu.make_async_copy(final.at[h, mine], out.at[:, out_columns(h)], lsem.at[9 + h]).start()
        for peer in peers:
            pltpu.make_async_remote_copy(
                src_ref=final.at[h, pl.ds(pl.multiple_of(peer * rows, rows), rows)],
                dst_ref=out.at[:, out_columns(h)],
                send_sem=ao_s.at[h], recv_sem=ao_r.at[h],
                device_id=(patch, peer), device_id_type=MESH,
            ).start()

    order = (
        (0, 1), (0, 2), (0, 0), (1, 1), (1, 2), (1, 0),
        (0, 3), (2, 2), (2, 0), (1, 3), (2, 1), (2, 3),
    )
    plan = {
        0: lambda: (ready("V", 0), arrived("Q", "z", 0)),
        1: lambda: ([forward_z(t, 2) for t in "KV"], arrived("Q", "xz", 0)),
        2: lambda: (ready("K", 1), arrived("Q", "x", 1)),
        3: lambda: (
            ready("V", 1),
            [forward_x(t, 2) for t in "KV"],
            [forward_xz(t, 2) for t in "KV"],
            arrived("Q", "z", 1),
        ),
        4: lambda: arrived("Q", "xz", 1),
        5: take_fresh,
        6: lambda: (ready("K", 2), arrived("Q", "z", 2)),
        7: lambda: (ready("V", 2), arrived("Q", "xz", 2)),
        8: lambda: finish(0),
        9: lambda: arrived("Q", "x", 2),
        10: lambda: finish(1),
    }
    blk = ka.shape[2]

    def pick(s, values):
        r = values[0]
        for i, v in enumerate(values):
            r = jnp.where(s == i, v, r)
        return r

    def item(s):
        return pick(s, [h for h, _ in order]), pick(s, [j for _, j in order])

    def score(h, j, slot, b):
        k = ka[(j // 3) * 8 if b == 0 else b, h]
        s = lax.dot_general(
            k, qa[j, h], (((1,), (1,)), ((), ())), preferred_element_type=jnp.float32
        )
        scores[slot, b * blk : (b + 1) * blk] = s
        return jnp.max(s.reshape(blk // 8, 8, s.shape[1]), axis=0)

    def gather_values(h, j, slot, b, m):
        w = jnp.exp2((scores[slot, b * blk : (b + 1) * blk] - m) * SCALE)
        o = jnp.dot(
            va[(j // 3) * 8 if b == 0 else b, h], w.astype(jnp.bfloat16),
            preferred_element_type=jnp.float32,
        )
        return o, jnp.sum(w.reshape(blk // 8, 8, w.shape[1]), axis=0)

    def attend(now, later, slot, m8):
        m = jnp.max(m8, axis=0, keepdims=True)
        o, l8, new = 0.0, 0.0, None
        for b in range(8):
            o_b, l_b = gather_values(*now, slot, b, m)
            o, l8 = o + o_b, l8 + l_b
            if later is not None:
                top = score(*later, 1 - slot, b)
                new = top if new is None else jnp.maximum(new, top)
        l = jnp.sum(l8, axis=0, keepdims=True)
        return o * (1.0 / l), stats(m, l), new

    m8 = None
    for b in range(8):
        top = score(*order[0], 0, b)
        m8 = top if m8 is None else jnp.maximum(m8, top)

    def step(s, m8):
        for at, action in plan.items():
            pl.when(s == at)(lambda action=action: (action(), None)[1])
        h, j = item(s)
        o, t, m8 = attend((h, j), item(s + 1), s % 2, m8)

        for r in range(3):

            @pl.when(j == r)
            def _(r=r):
                send_o[h, r] = o.astype(jnp.bfloat16)
                send_t[h, r] = t
                start("O", r, h)
                start("T", r, h)

        @pl.when(j == 3)
        def _():
            part_o[h] = o
            part_t[h] = t

        return m8

    last = len(order) - 1
    m8 = lax.fori_loop(0, last, step, m8)
    o, t, _ = attend(order[last], None, last % 2, m8)
    part_o[nh - 1] = o
    part_t[nh - 1] = t
    finish(nh - 1)

    for h in range(nh):
        some = out.at[:, pl.ds(0, (uly - 1) * HD)]
        pltpu.make_async_copy(some, some, ao_r.at[h]).wait()
        pltpu.make_async_copy(some, some, ao_s.at[h]).wait()
        pltpu.make_async_copy(final.at[h, mine], out.at[:, out_columns(h)], lsem.at[9 + h]).wait()
    for n, dst in enumerate((qland, kland, vland)):
        whole = dst.at[pl.ds(0, (uly - 1) * rows)]
        pltpu.make_async_copy(whole, whole, a2a_s.at[n]).wait()
    pltpu.make_async_copy(kland, fresh.at[0], lsem.at[7]).wait()
    pltpu.make_async_copy(vland, fresh.at[1], lsem.at[8]).wait()
    for kind in KINDS:
        for h in range(nh):
            copy(kind, h).wait_send()


def local(queries, keys, values, stale_cache):
    rows, width = queries.shape
    _, patch_rows, cols = stale_cache.shape
    nh = cols // HD
    bf, f32 = jnp.bfloat16, jnp.float32
    n_copies = len(KINDS) * nh
    vm = pltpu.VMEM
    dma = pltpu.SemaphoreType.DMA
    return pl.pallas_call(
        kernel,
        out_shape=(
            jax.ShapeDtypeStruct((rows, width), bf),
            jax.ShapeDtypeStruct(stale_cache.shape, bf),
        ),
        in_specs=[pl.BlockSpec(memory_space=pl.ANY)] * 4,
        out_specs=(pl.BlockSpec(memory_space=pl.ANY),) * 2,
        scratch_shapes=[
            vm((9, nh, patch_rows, HD), bf),
            vm((9, nh, HD, patch_rows), bf),
            vm((4, nh, patch_rows, HD), bf),
            vm((patch_rows, cols), bf),
            vm((patch_rows, cols), bf),
            vm((patch_rows, cols), bf),
            vm((patch_rows, cols), bf),
            vm((2, 8 * patch_rows, patch_rows), f32),
            vm((nh, HD, patch_rows), f32),
            vm((nh, 8, patch_rows), f32),
            vm((nh, 3, HD, patch_rows), bf),
            vm((nh, 3, 8, patch_rows), f32),
            vm((nh, 3, HD, patch_rows), bf),
            vm((nh, 3, 8, patch_rows), f32),
            vm((nh, patch_rows, HD), bf),
            dma((n_copies,)),
            dma((n_copies,)),
            dma((3,)),
            dma((3,)),
            dma((nh,)),
            dma((nh,)),
            dma((9 + nh,)),
        ],
        compiler_params=pltpu.CompilerParams(
            collective_id=0, has_side_effects=True, vmem_limit_bytes=62 * 2**20
        ),
        cost_estimate=pl.CostEstimate(
            flops=4 * 8 * 4 * patch_rows**2 * cols,
            bytes_accessed=8 * patch_rows * cols,
            transcendentals=32 * patch_rows**2 * nh,
        ),
    )(queries, keys, values, stale_cache)


def solution(mesh):
    in_specs = (
        P(("patch", "uly"), None),
        P(("patch", "uly"), None),
        P(("patch", "uly"), None),
        P(None, "patch", "uly"),
    )
    out_specs = (P(("patch", "uly"), None), P(None, "patch", "uly"))
    return jax.shard_map(local, mesh=mesh, in_specs=in_specs, out_specs=out_specs, check_vma=False)
```

```python
import jax
import jax.numpy as jnp
from jax import lax
from jax.experimental import pallas as pl
from jax.experimental.pallas import tpu as pltpu
from jax.sharding import PartitionSpec as P

MESH = pl.DeviceIdType.MESH
HEADS = 48
HD = 128
SCALE = 1.4426950408889634 * HD**-0.5

KINDS = (
    [(t, r) for t in "KV" for r in ("z", "x", "s0", "xz", "s1", "s2", "s3")]
    + [("Q", r) for r in ("z", "x", "xz")]
    + [(t, r) for t in "OT" for r in (0, 1, 2)]
)
KIND_INDEX = {kind: i for i, kind in enumerate(KINDS)}


def kernel(
    q_hbm, k_hbm, v_hbm, stale, out, fresh,
    ka, va, qa, qland, kland, vland, stale_v,
    scores, part_o, part_t, send_o, send_t, got_o, got_t, final,
    ssem, rsem, a2a_s, a2a_r, ao_s, ao_r, lsem,
):
    rows, width = q_hbm.shape
    uly = width // qland.shape[1]
    nh = qland.shape[1] // HD
    patch = lax.axis_index("patch")
    me = lax.axis_index("uly")
    core = patch % 2
    x = (patch // 2) % 4
    zh = patch // 8

    def at_patch(zh_, x_, core_):
        return ((zh_ * 4 + x_) * 2 + core_, me)

    sib = at_patch(zh, x, 1 - core)

    def flip(i, crossed):
        return (i + 1 - 2 * (i % 2)) * (1 - crossed) + (3 - i) * crossed

    def partner(r, crossed):
        return at_patch(
            flip(zh, crossed) if "z" in r else zh, flip(x, crossed) if "x" in r else x, core
        )

    def copy(kind, h):
        t, r = kind
        if t in "KV":
            slots = ka if t == "K" else va
            src, dst, to = {
                "z": (0, 1, "z"),
                "x": (0, 2, "x"),
                "s0": (0, 4, ""),
                "xz": (1, 3, "x"),
                "s1": (1, 5, ""),
                "s2": (2, 6, ""),
                "s3": (3, 7, ""),
            }[r]
            if t == "K" and src == 0:
                src = stale.at[0, :, pl.ds(h * HD, HD)]
            else:
                src = slots.at[src, h]
            dst = slots.at[dst, h]
            to = partner(to, h % 2) if to else sib
        elif t == "Q":
            src, dst = qa.at[3, h], qa.at[("xz", "x", "z").index(r), h]
            to = partner(r, 1 - h % 2)
        else:
            src = (send_o if t == "O" else send_t).at[h, r]
            dst = (got_o if t == "O" else got_t).at[h, r]
            to = partner(("xz", "x", "z")[r], 1 - h % 2)
        i = KIND_INDEX[kind] * nh + h
        return pltpu.make_async_remote_copy(
            src_ref=src, dst_ref=dst, send_sem=ssem.at[i], recv_sem=rsem.at[i],
            device_id=to, device_id_type=MESH,
        )

    def start(t, r, h):
        copy((t, r), h).start()

    def arrived(t, r, h):
        copy((t, r), h).wait_recv()

    barrier = pltpu.get_barrier_semaphore()
    ring = uly // 2
    steps = [(dz, dy) for dz in range(2) for dy in range(ring) if dz + dy]
    steps.sort(key=lambda d: -d[0] - min(d[1], ring - d[1]))
    peers = [((me // ring + dz) % 2) * ring + (me + dy) % ring for dz, dy in steps]
    for peer in peers:
        pl.semaphore_signal(barrier, inc=1, device_id=(patch, peer), device_id_type=MESH)
    near = [sib] + [partner(r, crossed) for r in ("z", "x", "xz") for crossed in (0, 1)]
    for to in near:
        pl.semaphore_signal(barrier, inc=1, device_id=to, device_id_type=MESH)

    cut = pl.ds(pl.multiple_of(me * nh * HD, HD), nh * HD)
    mine = pl.ds(pl.multiple_of(me * rows, rows), rows)
    local = [pltpu.make_async_copy(stale.at[1], stale_v, lsem.at[0])]
    for i, (src, dst) in enumerate(((q_hbm, qland), (k_hbm, kland), (v_hbm, vland))):
        local.append(pltpu.make_async_copy(src.at[:, cut], dst.at[mine], lsem.at[1 + i]))
    for h in range(nh):
        local.append(
            pltpu.make_async_copy(stale.at[0, :, pl.ds(h * HD, HD)], ka.at[0, h], lsem.at[4 + h])
        )
    for c in local:
        c.start()

    pl.semaphore_wait(barrier, uly - 1 + len(near))

    def exchange(n, src, dst):
        for peer in peers:
            pltpu.make_async_remote_copy(
                src_ref=src.at[:, pl.ds(pl.multiple_of(peer * nh * HD, HD), nh * HD)],
                dst_ref=dst.at[mine],
                send_sem=a2a_s.at[n], recv_sem=a2a_r.at[n],
                device_id=(patch, peer), device_id_type=MESH,
            ).start()

    def exchanged(n, dst):
        whole = dst.at[pl.ds(0, (uly - 1) * rows)]
        pltpu.make_async_copy(whole, whole, a2a_r.at[n]).wait()
        local[1 + n].wait()

    def forward_z(t, h):
        arrived(t, "z", h)
        start(t, "xz", h)
        start(t, "s1", h)

    def forward_x(t, h):
        arrived(t, "x", h)
        start(t, "s2", h)

    def forward_xz(t, h):
        arrived(t, "xz", h)
        start(t, "s3", h)

    def ready(t, h):
        for r in ("s0", "s1", "s2", "s3"):
            arrived(t, r, h)

    def start_both(r, h):
        for t in "KV":
            start(t, r, h)

    def start_query(h):
        qa[3, h] = qland[:, h * HD : (h + 1) * HD]
        for r in ("xz", "z", "x"):
            start("Q", r, h)

    exchange(0, q_hbm, qland)
    for h in (0, 1):
        for r in ("z", "x", "s0"):
            start("K", r, h)
    local[0].wait()
    for h in range(nh):
        va[0, h] = stale_v[:, h * HD : (h + 1) * HD].T
        if h < 2:
            for r in ("z", "x", "s0"):
                start("V", r, h)
    for h in range(nh):
        local[4 + h].wait()
    for t in "KV":
        forward_z(t, 0)
    start_both("z", 2)
    for t in "KV":
        forward_z(t, 1)
    for h in (0, 1):
        for t in "KV":
            forward_x(t, h)
    exchanged(0, qland)
    start_query(0)
    start_query(1)
    start_query(2)
    for t in "KV":
        forward_xz(t, 0)
    start_both("x", 2)
    start_both("s0", 2)
    for t in "KV":
        forward_xz(t, 1)
    ready("K", 0)
    arrived("Q", "x", 0)

    def take_fresh():
        exchanged(1, kland)
        exchanged(2, vland)
        pltpu.make_async_copy(kland, fresh.at[0], lsem.at[7]).start()
        pltpu.make_async_copy(vland, fresh.at[1], lsem.at[8]).start()
        for h in range(nh):
            ka[8, h] = kland[:, h * HD : (h + 1) * HD]
            va[8, h] = vland[:, h * HD : (h + 1) * HD].T

    def stats(m, l):
        row = lax.broadcasted_iota(jnp.int32, (8, m.shape[1]), 0)
        return jnp.where(row < 4, jnp.broadcast_to(m, row.shape), jnp.broadcast_to(l, row.shape))

    def out_columns(h):
        return pl.ds(pl.multiple_of((me * nh + h) * HD, HD), HD)

    def finish(h):
        for r in range(3):
            arrived("O", r, h)
            arrived("T", r, h)
        ts = [part_t[h]] + [got_t[h, r] for r in range(3)]
        m = jnp.maximum(
            jnp.maximum(ts[0][0:1], ts[1][0:1]), jnp.maximum(ts[2][0:1], ts[3][0:1])
        )
        shares = [t[4:5] * jnp.exp2((t[0:1] - m) * SCALE) for t in ts]
        inverse = 1.0 / (shares[0] + shares[1] + shares[2] + shares[3])
        o = part_o[h] * (shares[0] * inverse)
        for r in range(3):
            o = o + got_o[h, r].astype(jnp.float32) * (shares[1 + r] * inverse)
        final[h] = o.T.astype(jnp.bfloat16)
        pltpu.make_async_copy(final.at[h, mine], out.at[:, out_columns(h)], lsem.at[9 + h]).start()
        for peer in peers:
            pltpu.make_async_remote_copy(
                src_ref=final.at[h, pl.ds(pl.multiple_of(peer * rows, rows), rows)],
                dst_ref=out.at[:, out_columns(h)],
                send_sem=ao_s.at[h], recv_sem=ao_r.at[h],
                device_id=(patch, peer), device_id_type=MESH,
            ).start()

    order = (
        (0, 1), (0, 2), (0, 0), (1, 1), (1, 2), (1, 0),
        (2, 2), (2, 0), (0, 3), (1, 3), (2, 1), (2, 3),
    )
    plan = {
        0: lambda: (
            ready("V", 0),
            arrived("Q", "z", 0),
            exchange(1, k_hbm, kland),
            exchange(2, v_hbm, vland),
        ),
        1: lambda: ([forward_z(t, 2) for t in "KV"], arrived("Q", "xz", 0)),
        2: lambda: (ready("K", 1), arrived("Q", "x", 1)),
        3: lambda: (
            ready("V", 1),
            [forward_x(t, 2) for t in "KV"],
            [forward_xz(t, 2) for t in "KV"],
            arrived("Q", "z", 1),
        ),
        4: lambda: arrived("Q", "xz", 1),
        5: lambda: (ready("K", 2), arrived("Q", "z", 2)),
        6: lambda: (ready("V", 2), arrived("Q", "xz", 2)),
        7: take_fresh,
        9: lambda: (arrived("Q", "x", 2), finish(0)),
        10: lambda: finish(1),
    }
    blk = ka.shape[2]

    def pick(s, values):
        r = values[0]
        for i, v in enumerate(values):
            r = jnp.where(s == i, v, r)
        return r

    def item(s):
        return pick(s, [h for h, _ in order]), pick(s, [j for _, j in order])

    def score(h, j, slot, b):
        k = ka[(j // 3) * 8 if b == 0 else b, h]
        s = lax.dot_general(
            k, qa[j, h], (((1,), (1,)), ((), ())), preferred_element_type=jnp.float32
        )
        scores[slot, b * blk : (b + 1) * blk] = s
        return jnp.max(s.reshape(blk // 8, 8, s.shape[1]), axis=0)

    def gather_values(h, j, slot, b, m):
        w = jnp.exp2((scores[slot, b * blk : (b + 1) * blk] - m) * SCALE)
        o = jnp.dot(
            va[(j // 3) * 8 if b == 0 else b, h], w.astype(jnp.bfloat16),
            preferred_element_type=jnp.float32,
        )
        return o, jnp.sum(w.reshape(blk // 8, 8, w.shape[1]), axis=0)

    def attend(now, later, slot, m8):
        m = jnp.max(m8, axis=0, keepdims=True)
        o, l8, new = 0.0, 0.0, None
        for b in range(8):
            o_b, l_b = gather_values(*now, slot, b, m)
            o, l8 = o + o_b, l8 + l_b
            if later is not None:
                top = score(*later, 1 - slot, b)
                new = top if new is None else jnp.maximum(new, top)
        l = jnp.sum(l8, axis=0, keepdims=True)
        return o * (1.0 / l), stats(m, l), new

    m8 = None
    for b in range(8):
        top = score(*order[0], 0, b)
        m8 = top if m8 is None else jnp.maximum(m8, top)

    def step(s, m8):
        for at, action in plan.items():
            pl.when(s == at)(lambda action=action: (action(), None)[1])
        h, j = item(s)
        o, t, m8 = attend((h, j), item(s + 1), s % 2, m8)

        for r in range(3):

            @pl.when(j == r)
            def _(r=r):
                send_o[h, r] = o.astype(jnp.bfloat16)
                send_t[h, r] = t
                start("O", r, h)
                start("T", r, h)

        @pl.when(j == 3)
        def _():
            part_o[h] = o
            part_t[h] = t

        return m8

    last = len(order) - 1
    m8 = lax.fori_loop(0, last, step, m8)
    o, t, _ = attend(order[last], None, last % 2, m8)
    part_o[nh - 1] = o
    part_t[nh - 1] = t
    finish(nh - 1)

    for h in range(nh):
        some = out.at[:, pl.ds(0, (uly - 1) * HD)]
        pltpu.make_async_copy(some, some, ao_r.at[h]).wait()
        pltpu.make_async_copy(some, some, ao_s.at[h]).wait()
        pltpu.make_async_copy(final.at[h, mine], out.at[:, out_columns(h)], lsem.at[9 + h]).wait()
    for n, dst in enumerate((qland, kland, vland)):
        whole = dst.at[pl.ds(0, (uly - 1) * rows)]
        pltpu.make_async_copy(whole, whole, a2a_s.at[n]).wait()
    pltpu.make_async_copy(kland, fresh.at[0], lsem.at[7]).wait()
    pltpu.make_async_copy(vland, fresh.at[1], lsem.at[8]).wait()
    for kind in KINDS:
        for h in range(nh):
            copy(kind, h).wait_send()


def copy_out(*refs):
    sems = refs[-1]
    inward = [pltpu.make_async_copy(refs[i], refs[4 + i], sems.at[i]) for i in range(2)]
    outward = [pltpu.make_async_copy(refs[4 + i], refs[2 + i], sems.at[2 + i]) for i in range(2)]
    for c in inward:
        c.start()
    for c, d in zip(inward, outward):
        c.wait()
        d.start()
    for d in outward:
        d.wait()


def local(queries, keys, values, stale_cache):
    rows, width = queries.shape
    _, patch_rows, cols = stale_cache.shape
    nh = cols // HD
    bf, f32 = jnp.bfloat16, jnp.float32
    n_copies = len(KINDS) * nh
    vm = pltpu.VMEM
    dma = pltpu.SemaphoreType.DMA
    results = pl.pallas_call(
        kernel,
        out_shape=(
            jax.ShapeDtypeStruct((rows, width), bf),
            jax.ShapeDtypeStruct(stale_cache.shape, bf),
        ),
        in_specs=[pl.BlockSpec(memory_space=pl.ANY)] * 4,
        out_specs=(pl.BlockSpec(memory_space=pl.ANY),) * 2,
        scratch_shapes=[
            vm((9, nh, patch_rows, HD), bf),
            vm((9, nh, HD, patch_rows), bf),
            vm((4, nh, patch_rows, HD), bf),
            vm((patch_rows, cols), bf),
            vm((patch_rows, cols), bf),
            vm((patch_rows, cols), bf),
            vm((patch_rows, cols), bf),
            vm((2, 8 * patch_rows, patch_rows), f32),
            vm((nh, HD, patch_rows), f32),
            vm((nh, 8, patch_rows), f32),
            vm((nh, 3, HD, patch_rows), bf),
            vm((nh, 3, 8, patch_rows), f32),
            vm((nh, 3, HD, patch_rows), bf),
            vm((nh, 3, 8, patch_rows), f32),
            vm((nh, patch_rows, HD), bf),
            dma((n_copies,)),
            dma((n_copies,)),
            dma((3,)),
            dma((3,)),
            dma((nh,)),
            dma((nh,)),
            dma((9 + nh,)),
        ],
        compiler_params=pltpu.CompilerParams(
            collective_id=0, has_side_effects=True, vmem_limit_bytes=62 * 2**20
        ),
        cost_estimate=pl.CostEstimate(
            flops=4 * 8 * 4 * patch_rows**2 * cols,
            bytes_accessed=8 * patch_rows * cols,
            transcendentals=32 * patch_rows**2 * nh,
        ),
    )(queries, keys, values, stale_cache)
    return pl.pallas_call(
        copy_out,
        out_shape=tuple(jax.ShapeDtypeStruct(r.shape, r.dtype) for r in results),
        in_specs=[pl.BlockSpec(memory_space=pl.ANY)] * 2,
        out_specs=(pl.BlockSpec(memory_space=pl.ANY),) * 2,
        scratch_shapes=[vm(r.shape, r.dtype) for r in results] + [dma((4,))],
        compiler_params=pltpu.CompilerParams(vmem_limit_bytes=62 * 2**20),
    )(*results)


def solution(mesh):
    in_specs = (
        P(("patch", "uly"), None),
        P(("patch", "uly"), None),
        P(("patch", "uly"), None),
        P(None, "patch", "uly"),
    )
    out_specs = (P(("patch", "uly"), None), P(None, "patch", "uly"))
    return jax.shard_map(local, mesh=mesh, in_specs=in_specs, out_specs=out_specs, check_vma=False)
```

```python
import jax
import jax.numpy as jnp
from jax import lax
from jax.experimental import pallas as pl
from jax.experimental.pallas import tpu as pltpu
from jax.sharding import PartitionSpec as P

MESH = pl.DeviceIdType.MESH
HEADS = 48
HD = 128
SCALE = 1.4426950408889634 * HD**-0.5

KINDS = (
    [(t, r) for t in "KV" for r in ("z", "x", "s0", "xz", "s1", "s2", "s3")]
    + [("Q", r) for r in ("z", "x", "xz")]
    + [(t, r) for t in "OT" for r in (0, 1, 2)]
)
KIND_INDEX = {kind: i for i, kind in enumerate(KINDS)}


def kernel(
    q_hbm, k_hbm, v_hbm, stale, out, fresh,
    ka, va, qa, qland, kland, vland, stale_v,
    scores, part_o, part_t, send_o, send_t, got_o, got_t, final,
    ssem, rsem, a2a_s, a2a_r, ao_s, ao_r, lsem,
):
    rows, width = q_hbm.shape
    uly = width // qland.shape[1]
    nh = qland.shape[1] // HD
    patch = lax.axis_index("patch")
    me = lax.axis_index("uly")
    core = patch % 2
    x = (patch // 2) % 4
    zh = patch // 8

    def at_patch(zh_, x_, core_):
        return ((zh_ * 4 + x_) * 2 + core_, me)

    sib = at_patch(zh, x, 1 - core)

    def flip(i, crossed):
        return (i + 1 - 2 * (i % 2)) * (1 - crossed) + (3 - i) * crossed

    def partner(r, crossed):
        return at_patch(
            flip(zh, crossed) if "z" in r else zh, flip(x, crossed) if "x" in r else x, core
        )

    def copy(kind, h):
        t, r = kind
        if t in "KV":
            slots = ka if t == "K" else va
            src, dst, to = {
                "z": (0, 1, "z"),
                "x": (0, 2, "x"),
                "s0": (0, 4, ""),
                "xz": (1, 3, "x"),
                "s1": (1, 5, ""),
                "s2": (2, 6, ""),
                "s3": (3, 7, ""),
            }[r]
            if t == "K" and src == 0:
                src = stale.at[0, :, pl.ds(h * HD, HD)]
            else:
                src = slots.at[src, h]
            dst = slots.at[dst, h]
            to = partner(to, h % 2) if to else sib
        elif t == "Q":
            src, dst = qa.at[3, h], qa.at[("xz", "x", "z").index(r), h]
            to = partner(r, 1 - h % 2)
        else:
            src = (send_o if t == "O" else send_t).at[h, r]
            dst = (got_o if t == "O" else got_t).at[h, r]
            to = partner(("xz", "x", "z")[r], 1 - h % 2)
        i = KIND_INDEX[kind] * nh + h
        return pltpu.make_async_remote_copy(
            src_ref=src, dst_ref=dst, send_sem=ssem.at[i], recv_sem=rsem.at[i],
            device_id=to, device_id_type=MESH,
        )

    def start(t, r, h):
        copy((t, r), h).start()

    def arrived(t, r, h):
        copy((t, r), h).wait_recv()

    barrier = pltpu.get_barrier_semaphore()
    ring = uly // 2
    steps = [(dz, dy) for dz in range(2) for dy in range(ring) if dz + dy]
    steps.sort(key=lambda d: -d[0] - min(d[1], ring - d[1]))
    peers = [((me // ring + dz) % 2) * ring + (me + dy) % ring for dz, dy in steps]
    for peer in peers:
        pl.semaphore_signal(barrier, inc=1, device_id=(patch, peer), device_id_type=MESH)
    near = [sib] + [partner(r, crossed) for r in ("z", "x", "xz") for crossed in (0, 1)]
    for to in near:
        pl.semaphore_signal(barrier, inc=1, device_id=to, device_id_type=MESH)

    cut = pl.ds(pl.multiple_of(me * nh * HD, HD), nh * HD)
    mine = pl.ds(pl.multiple_of(me * rows, rows), rows)
    local = [pltpu.make_async_copy(stale.at[1], stale_v, lsem.at[0])]
    for i, (src, dst) in enumerate(((q_hbm, qland), (k_hbm, kland), (v_hbm, vland))):
        local.append(pltpu.make_async_copy(src.at[:, cut], dst.at[mine], lsem.at[1 + i]))
    for h in range(nh):
        local.append(
            pltpu.make_async_copy(stale.at[0, :, pl.ds(h * HD, HD)], ka.at[0, h], lsem.at[4 + h])
        )
    for c in local:
        c.start()

    pl.semaphore_wait(barrier, uly - 1 + len(near))

    def exchange(n, src, dst):
        for peer in peers:
            pltpu.make_async_remote_copy(
                src_ref=src.at[:, pl.ds(pl.multiple_of(peer * nh * HD, HD), nh * HD)],
                dst_ref=dst.at[mine],
                send_sem=a2a_s.at[n], recv_sem=a2a_r.at[n],
                device_id=(patch, peer), device_id_type=MESH,
            ).start()

    def exchanged(n, dst):
        whole = dst.at[pl.ds(0, (uly - 1) * rows)]
        pltpu.make_async_copy(whole, whole, a2a_r.at[n]).wait()
        local[1 + n].wait()

    def forward_z(t, h):
        arrived(t, "z", h)
        start(t, "xz", h)
        start(t, "s1", h)

    def forward_x(t, h):
        arrived(t, "x", h)
        start(t, "s2", h)

    def forward_xz(t, h):
        arrived(t, "xz", h)
        start(t, "s3", h)

    def ready(t, h):
        for r in ("s0", "s1", "s2", "s3"):
            arrived(t, r, h)

    def start_both(r, h):
        for t in "KV":
            start(t, r, h)

    def start_query(h):
        qa[3, h] = qland[:, h * HD : (h + 1) * HD]
        for r in ("xz", "z", "x"):
            start("Q", r, h)

    exchange(0, q_hbm, qland)
    for h in (0, 1):
        for r in ("z", "x", "s0"):
            start("K", r, h)
    local[0].wait()
    for h in range(nh):
        va[0, h] = stale_v[:, h * HD : (h + 1) * HD].T
        if h < 2:
            for r in ("z", "x", "s0"):
                start("V", r, h)
    for h in range(nh):
        local[4 + h].wait()
    for t in "KV":
        forward_z(t, 0)
    start_both("z", 2)
    for t in "KV":
        forward_z(t, 1)
    for h in (0, 1):
        for t in "KV":
            forward_x(t, h)
    exchanged(0, qland)
    start_query(0)
    start_query(1)
    start_query(2)
    for t in "KV":
        forward_xz(t, 0)
    start_both("x", 2)
    start_both("s0", 2)
    for t in "KV":
        forward_xz(t, 1)
    ready("K", 0)
    arrived("Q", "x", 0)

    def take_fresh():
        exchanged(1, kland)
        exchanged(2, vland)
        pltpu.make_async_copy(kland, fresh.at[0], lsem.at[7]).start()
        pltpu.make_async_copy(vland, fresh.at[1], lsem.at[8]).start()
        for h in range(nh):
            ka[8, h] = kland[:, h * HD : (h + 1) * HD]
            va[8, h] = vland[:, h * HD : (h + 1) * HD].T

    def stats(m, l):
        row = lax.broadcasted_iota(jnp.int32, (8, m.shape[1]), 0)
        return jnp.where(row < 4, jnp.broadcast_to(m, row.shape), jnp.broadcast_to(l, row.shape))

    def out_columns(h):
        return pl.ds(pl.multiple_of((me * nh + h) * HD, HD), HD)

    def finish(h):
        for r in range(3):
            arrived("O", r, h)
            arrived("T", r, h)
        ts = [part_t[h]] + [got_t[h, r] for r in range(3)]
        m = jnp.maximum(
            jnp.maximum(ts[0][0:1], ts[1][0:1]), jnp.maximum(ts[2][0:1], ts[3][0:1])
        )
        shares = [t[4:5] * jnp.exp2((t[0:1] - m) * SCALE) for t in ts]
        inverse = 1.0 / (shares[0] + shares[1] + shares[2] + shares[3])
        o = part_o[h] * (shares[0] * inverse)
        for r in range(3):
            o = o + got_o[h, r].astype(jnp.float32) * (shares[1 + r] * inverse)
        final[h] = o.T.astype(jnp.bfloat16)
        pltpu.make_async_copy(final.at[h, mine], out.at[:, out_columns(h)], lsem.at[9 + h]).start()
        for peer in peers:
            pltpu.make_async_remote_copy(
                src_ref=final.at[h, pl.ds(pl.multiple_of(peer * rows, rows), rows)],
                dst_ref=out.at[:, out_columns(h)],
                send_sem=ao_s.at[h], recv_sem=ao_r.at[h],
                device_id=(patch, peer), device_id_type=MESH,
            ).start()

    order = (
        (0, 1), (0, 2), (0, 0), (1, 1), (1, 2), (1, 0),
        (2, 2), (2, 0), (0, 3), (2, 1), (1, 3), (2, 3),
    )
    plan = {
        0: lambda: (
            ready("V", 0),
            arrived("Q", "z", 0),
            exchange(1, k_hbm, kland),
            exchange(2, v_hbm, vland),
        ),
        1: lambda: ([forward_z(t, 2) for t in "KV"], arrived("Q", "xz", 0)),
        2: lambda: (ready("K", 1), arrived("Q", "x", 1)),
        3: lambda: (
            ready("V", 1),
            [forward_x(t, 2) for t in "KV"],
            [forward_xz(t, 2) for t in "KV"],
            arrived("Q", "z", 1),
        ),
        4: lambda: arrived("Q", "xz", 1),
        5: lambda: (ready("K", 2), arrived("Q", "z", 2)),
        6: lambda: (ready("V", 2), arrived("Q", "xz", 2)),
        7: take_fresh,
        8: lambda: arrived("Q", "x", 2),
        9: lambda: finish(0),
    }
    blk = ka.shape[2]

    def pick(s, values):
        r = values[0]
        for i, v in enumerate(values):
            r = jnp.where(s == i, v, r)
        return r

    def item(s):
        return pick(s, [h for h, _ in order]), pick(s, [j for _, j in order])

    def score(h, j, slot, b):
        k = ka[(j // 3) * 8 if b == 0 else b, h]
        s = lax.dot_general(
            k, qa[j, h], (((1,), (1,)), ((), ())), preferred_element_type=jnp.float32
        )
        scores[slot, b * blk : (b + 1) * blk] = s
        return jnp.max(s.reshape(blk // 8, 8, s.shape[1]), axis=0)

    def gather_values(h, j, slot, b, m):
        w = jnp.exp2((scores[slot, b * blk : (b + 1) * blk] - m) * SCALE)
        o = jnp.dot(
            va[(j // 3) * 8 if b == 0 else b, h], w.astype(jnp.bfloat16),
            preferred_element_type=jnp.float32,
        )
        return o, jnp.sum(w.reshape(blk // 8, 8, w.shape[1]), axis=0)

    def attend(now, later, slot, m8):
        m = jnp.max(m8, axis=0, keepdims=True)
        o, l8, new = 0.0, 0.0, None
        for b in range(8):
            o_b, l_b = gather_values(*now, slot, b, m)
            o, l8 = o + o_b, l8 + l_b
            if later is not None:
                top = score(*later, 1 - slot, b)
                new = top if new is None else jnp.maximum(new, top)
        l = jnp.sum(l8, axis=0, keepdims=True)
        return o * (1.0 / l), stats(m, l), new

    m8 = None
    for b in range(8):
        top = score(*order[0], 0, b)
        m8 = top if m8 is None else jnp.maximum(m8, top)

    def step(s, m8):
        for at, action in plan.items():
            pl.when(s == at)(lambda action=action: (action(), None)[1])
        h, j = item(s)
        o, t, m8 = attend((h, j), item(s + 1), s % 2, m8)

        for r in range(3):

            @pl.when(j == r)
            def _(r=r):
                send_o[h, r] = o.astype(jnp.bfloat16)
                send_t[h, r] = t
                start("O", r, h)
                start("T", r, h)

        @pl.when(j == 3)
        def _():
            part_o[h] = o
            part_t[h] = t

        return m8

    last = len(order) - 1
    m8 = lax.fori_loop(0, last, step, m8)
    finish(1)
    o, t, _ = attend(order[last], None, last % 2, m8)
    part_o[nh - 1] = o
    part_t[nh - 1] = t
    finish(nh - 1)

    for h in range(nh):
        some = out.at[:, pl.ds(0, (uly - 1) * HD)]
        pltpu.make_async_copy(some, some, ao_r.at[h]).wait()
        pltpu.make_async_copy(some, some, ao_s.at[h]).wait()
        pltpu.make_async_copy(final.at[h, mine], out.at[:, out_columns(h)], lsem.at[9 + h]).wait()
    for n, dst in enumerate((qland, kland, vland)):
        whole = dst.at[pl.ds(0, (uly - 1) * rows)]
        pltpu.make_async_copy(whole, whole, a2a_s.at[n]).wait()
    pltpu.make_async_copy(kland, fresh.at[0], lsem.at[7]).wait()
    pltpu.make_async_copy(vland, fresh.at[1], lsem.at[8]).wait()
    for kind in KINDS:
        for h in range(nh):
            copy(kind, h).wait_send()


def copy_out(*refs):
    sems = refs[-1]
    inward = [pltpu.make_async_copy(refs[i], refs[4 + i], sems.at[i]) for i in range(2)]
    outward = [pltpu.make_async_copy(refs[4 + i], refs[2 + i], sems.at[2 + i]) for i in range(2)]
    for c in inward:
        c.start()
    for c, d in zip(inward, outward):
        c.wait()
        d.start()
    for d in outward:
        d.wait()


def local(queries, keys, values, stale_cache):
    rows, width = queries.shape
    _, patch_rows, cols = stale_cache.shape
    nh = cols // HD
    bf, f32 = jnp.bfloat16, jnp.float32
    n_copies = len(KINDS) * nh
    vm = pltpu.VMEM
    dma = pltpu.SemaphoreType.DMA
    results = pl.pallas_call(
        kernel,
        out_shape=(
            jax.ShapeDtypeStruct((rows, width), bf),
            jax.ShapeDtypeStruct(stale_cache.shape, bf),
        ),
        in_specs=[pl.BlockSpec(memory_space=pl.ANY)] * 4,
        out_specs=(pl.BlockSpec(memory_space=pl.ANY),) * 2,
        scratch_shapes=[
            vm((9, nh, patch_rows, HD), bf),
            vm((9, nh, HD, patch_rows), bf),
            vm((4, nh, patch_rows, HD), bf),
            vm((patch_rows, cols), bf),
            vm((patch_rows, cols), bf),
            vm((patch_rows, cols), bf),
            vm((patch_rows, cols), bf),
            vm((2, 8 * patch_rows, patch_rows), f32),
            vm((nh, HD, patch_rows), f32),
            vm((nh, 8, patch_rows), f32),
            vm((nh, 3, HD, patch_rows), bf),
            vm((nh, 3, 8, patch_rows), f32),
            vm((nh, 3, HD, patch_rows), bf),
            vm((nh, 3, 8, patch_rows), f32),
            vm((nh, patch_rows, HD), bf),
            dma((n_copies,)),
            dma((n_copies,)),
            dma((3,)),
            dma((3,)),
            dma((nh,)),
            dma((nh,)),
            dma((9 + nh,)),
        ],
        compiler_params=pltpu.CompilerParams(
            collective_id=0, has_side_effects=True, vmem_limit_bytes=62 * 2**20
        ),
        cost_estimate=pl.CostEstimate(
            flops=4 * 8 * 4 * patch_rows**2 * cols,
            bytes_accessed=8 * patch_rows * cols,
            transcendentals=32 * patch_rows**2 * nh,
        ),
    )(queries, keys, values, stale_cache)
    return pl.pallas_call(
        copy_out,
        out_shape=tuple(jax.ShapeDtypeStruct(r.shape, r.dtype) for r in results),
        in_specs=[pl.BlockSpec(memory_space=pl.ANY)] * 2,
        out_specs=(pl.BlockSpec(memory_space=pl.ANY),) * 2,
        scratch_shapes=[vm(r.shape, r.dtype) for r in results] + [dma((4,))],
        compiler_params=pltpu.CompilerParams(vmem_limit_bytes=62 * 2**20),
    )(*results)


def solution(mesh):
    in_specs = (
        P(("patch", "uly"), None),
        P(("patch", "uly"), None),
        P(("patch", "uly"), None),
        P(None, "patch", "uly"),
    )
    out_specs = (P(("patch", "uly"), None), P(None, "patch", "uly"))
    return jax.shard_map(local, mesh=mesh, in_specs=in_specs, out_specs=out_specs, check_vma=False)
```
